512 devices in a mesh: gx: 32 (over x, z), gy: 16 (over y, core).
Axes of the slice: x: 4, y: 8, z: 8, core: 2. Of those that a mesh axis runs over, the one named last changes fastest.
Arguments:
- source: float32 [512, 256, 256], P('gx', 'gy'), may hold values from -12 to 12
- inv_density: float32 [512, 256, 256], P('gx', 'gy'), may hold values from 0.4 to 2.5
Outputs:
- pressure: float32 [512, 256, 256], P('gx', 'gy')
The draws below stay inside these ranges and needn't reach their ends.
All inputs are finite; a program needn't handle non-finite values.
Results may differ from the reference program's by a relative error of at most 0.0001.
Values sent between devices are 32-bit elements; how exact they have to be, the bound alone decides.
A program may use at most 128 MiB of HBM per device.

```python
import math
import jax
import jax.numpy as jnp
from jax import lax

CX = 16
CY = 16
NZ = 256
LEVELS = 4
NU_PRE = 2
NU_COARSE = 4
NU_POST = 2
NX = 512
NY = 256


def large_scale(key, shape):
    keys = jax.random.split(key, 4)
    low_x = max(1, NX // (4 * CX))
    high_x = max(low_x, NX // (2 * CX))
    low_y = max(1, NY // (4 * CY))
    high_y = max(low_y, NY // (2 * CY))
    waves_x = jax.random.randint(keys[0], (3,), low_x, high_x + 1)
    waves_y = jax.random.randint(keys[1], (3,), low_y, high_y + 1)
    phases = jax.random.uniform(keys[2], (3,), jnp.float32, 0.0, 2.0 * math.pi)
    amplitudes = jax.random.uniform(keys[3], (3,), jnp.float32, 0.5, 1.0)
    index_x = lax.broadcasted_iota(jnp.int32, shape, 0)
    index_y = lax.broadcasted_iota(jnp.int32, shape, 1)
    total = jnp.zeros(shape, jnp.float32)
    for mode in range(3):
        turns_x = (waves_x[mode] * index_x % NX).astype(jnp.float32) / NX
        turns_y = (waves_y[mode] * index_y % NY).astype(jnp.float32) / NY
        total = total + amplitudes[mode] * jnp.cos(2.0 * math.pi * (turns_x + turns_y) + phases[mode])
    return total


def draw_source(key, part):
    key = jax.random.fold_in(key, 11)
    keys = jax.random.split(key, 3)
    shape = (NX, NY, NZ)
    factor = jnp.exp(jax.random.uniform(keys[1], shape, jnp.float32, math.log(0.5), math.log(2.0)))
    layers = lax.broadcasted_iota(jnp.int32, shape, 2).astype(jnp.float32)
    profile = 0.5 + 0.5 * jnp.sin(math.pi * (layers + 0.5) / NZ)
    smooth_part = large_scale(keys[2], shape)
    rough = jnp.clip(jax.random.normal(keys[0], shape, jnp.float32), -3.0, 3.0)
    return rough * factor + smooth_part * profile


def steps_of(key, dims, cuts, smallest, high):
    gain = 1.0
    for axis_at, parts in cuts:
        heights = jax.random.uniform(jax.random.fold_in(jax.random.fold_in(key, 6), axis_at), (parts,), jnp.float32, smallest / len(cuts), high / len(cuts))
        gain = gain * jnp.repeat(jnp.exp(heights), dims[axis_at] // parts).reshape((-1,) + (1,) * (len(dims) - 1 - axis_at))
    return gain


def setup_inputs(seed: int = 0) -> dict:
    seeds = jax.random.split(jax.random.key(seed), 3)
    return {
        "source": draw_source(jax.random.fold_in(seeds[2], 71), 0),
        "inv_density": jnp.clip(jnp.exp(math.log(2.5) - 1.8325814 * jax.random.uniform(seeds[1], (NX, NY, NZ), jnp.float32) ** steps_of(seeds[1], (NX, NY, NZ), ((0, 32), (1, 16)), -0.2, 0.2)), 0.4, 2.5),
    }


aspect_ratio = 0.25


def coefficients(beta_ext, weight):
    centre = beta_ext[1:-1, 1:-1]
    to_east = weight * 0.5 * (centre + beta_ext[2:, 1:-1])
    to_west = weight * 0.5 * (centre + beta_ext[:-2, 1:-1])
    to_north = weight * 0.5 * (centre + beta_ext[1:-1, 2:])
    to_south = weight * 0.5 * (centre + beta_ext[1:-1, :-2])
    upward = aspect_ratio * 0.5 * (centre + jnp.concatenate([centre[:, :, 1:], centre[:, :, -1:]], axis=2))
    downward = aspect_ratio * 0.5 * (centre + jnp.concatenate([centre[:, :, :1], centre[:, :, :-1]], axis=2))
    central = to_east + to_west + to_north + to_south + upward + downward
    return (to_east, to_west, to_north, to_south, upward, downward, central)


def neighbours(coeffs, extended):
    inner_part = extended[1:-1, 1:-1]
    zeros_layer = jnp.zeros_like(inner_part[:, :, :1])
    higher = jnp.concatenate([inner_part[:, :, 1:], zeros_layer], axis=2)
    beneath = jnp.concatenate([zeros_layer, inner_part[:, :, :-1]], axis=2)
    return (coeffs[0] * extended[2:, 1:-1] + coeffs[1] * extended[:-2, 1:-1]
            + coeffs[2] * extended[1:-1, 2:] + coeffs[3] * extended[1:-1, :-2]
            + coeffs[4] * higher + coeffs[5] * beneath)


def parity(shape):
    total = (lax.broadcasted_iota(jnp.int32, shape, 0) + lax.broadcasted_iota(jnp.int32, shape, 1)
             + lax.broadcasted_iota(jnp.int32, shape, 2))
    return total % 2 == 0


def wrapped(values):
    return jnp.pad(values, ((1, 1), (1, 1), (0, 0)), mode="wrap")


def restrict(values):
    return values.reshape(values.shape[0] // 2, 2, values.shape[1] // 2, 2, values.shape[2]).mean(axis=(1, 3))


def prolong(values):
    return jnp.repeat(jnp.repeat(values, 2, axis=0), 2, axis=1)


def smooth(pressure, source, coeffs, sweeps):
    red_cells = parity(pressure.shape)
    for sweep_index in range(sweeps):
        for colour in (red_cells, jnp.logical_not(red_cells)):
            beside_all = neighbours(coeffs, wrapped(pressure))
            pressure = jnp.where(colour, (source + beside_all) / coeffs[6], pressure)
    return pressure


def reference(source, inv_density):
    sources = [source]
    beta_levels = [inv_density]
    fields = []
    pressure = source
    for level_index in range(LEVELS):
        coeffs = coefficients(wrapped(beta_levels[level_index]), 0.25 ** level_index)
        sweeps = NU_COARSE if level_index == LEVELS - 1 else NU_PRE
        pressure = smooth(jnp.zeros_like(sources[level_index]), sources[level_index], coeffs, sweeps)
        if level_index < LEVELS - 1:
            fields.append(pressure)
            leftover = sources[level_index] - (coeffs[6] * pressure - neighbours(coeffs, wrapped(pressure)))
            sources.append(restrict(leftover))
            beta_levels.append(restrict(beta_levels[level_index]))
    for level_index in range(LEVELS - 2, -1, -1):
        coeffs = coefficients(wrapped(beta_levels[level_index]), 0.25 ** level_index)
        pressure = fields[level_index] + prolong(pressure)
        pressure = smooth(pressure, sources[level_index], coeffs, NU_POST)
    return pressure
```

```python
import jax
import jax.numpy as jnp
from jax import lax
from jax.experimental import pallas as pl
from jax.experimental.pallas import tpu as pltpu
from jax.sharding import PartitionSpec as P


MESH = pl.DeviceIdType.MESH
N = (16, 8, 4, 2)
HX = (6, 8, 8, 8)
HY = (6, 10, 10, 8)
XE = (28, 24, 20, 18)
YE = (32, 32, 32, 24)
WH = (0.5, 0.125, 0.03125, 0.0078125)
WV = 0.125
LANES = 128


def spread(n, radius, keep=None):
    out = []
    reach = -(-radius // n)
    for a in range(-reach, reach + 1):
        for b in range(-reach, reach + 1):
            gap_x = (abs(a) - 1) * n + 1 if a else 0
            gap_y = (abs(b) - 1) * n + 1 if b else 0
            if (a, b) == (0, 0) or gap_x + gap_y > radius:
                continue
            if keep is not None and not keep(a, b):
                continue
            rx, ry = radius - gap_y, radius - gap_x
            x0, x1 = max(-a * n, -rx), min(-a * n + n, n + rx)
            y0, y1 = max(-b * n, -ry), min(-b * n + n, n + ry)
            out.append((a, b, x0, x1 - x0, y0, y1 - y0))
    return out


def near(a, b):
    return max(abs(a), abs(b)) == 1


def far(a, b):
    return max(abs(a), abs(b)) > 1


GROUPS = {
    "b0": (0, 2, spread(16, 4)),
    "e0": (0, 2, spread(16, 5)),
    "e1": (1, 2, spread(8, 7)),
    "e2": (2, 2, spread(4, 8)),
    "e3": (3, 2, spread(2, 7)),
    "f0": (0, 1, spread(16, 4)),
    "b1": (1, 2, spread(8, 6)),
    "f1": (1, 1, spread(8, 7)),
    "b2": (2, 2, spread(4, 8, near)),
    "b2far": (2, 2, spread(4, 7, far)),
    "f2": (2, 1, spread(4, 8)),
    "b3": (3, 2, spread(2, 6)),
    "f3": (3, 1, spread(2, 6)),
}
NAMES = tuple(GROUPS)
COUNT = {k: c * sum(m[3] * m[5] for m in msgs) for k, (_, c, msgs) in GROUPS.items()}
MOST = -(-max(COUNT.values()) // 8) * 8
PARTNERS = sorted({m[:2] for _, _, msgs in GROUPS.values() for m in msgs})


def rows(x0, nx, body, group=4):
    steps = nx // group
    if steps > 1:

        def step(i, carry):
            for j in range(group):
                body(x0 + i * group + j, (x0 + j) % 2)
            return carry

        lax.fori_loop(0, steps, step, 0)
        done = steps * group
    else:
        done = 0
    for j in range(done, nx):
        body(x0 + j, (x0 + j) % 2)


def odd_rows(n, offset):
    return (lax.broadcasted_iota(jnp.int32, (n, LANES), 0) + offset) % 2 == 1


def kernel(gx_size, gy_size, src_ref, inv_ref, out_ref, *scratch):
    (e0, e1, e2, e3, b0, b1, b2, b3, p0, p1, p2, p3, q0, q1, q2, q3, d0, d1, d2, d3,
     g0, g1, g2, f0, f1, f2, f3, b2w, res, dummy, send_sem, recv_sem) = scratch
    beta, b, p, q, inv = (e0, e1, e2, e3), (b0, b1, b2, b3), (p0, p1, p2, p3), (q0, q1, q2, q3), (d0, d1, d2, d3)
    diag, field = (g0, g1, g2), (f0, f1, f2, f3)
    sent = {"b0": b0, "e0": e0, "e1": e1, "e2": e2, "e3": e3, "f0": f0, "b1": b1, "f1": f1,
            "b2": b2, "b2far": b2, "f2": f2, "b3": b3, "f3": f3}
    landed = dict(sent, b2far=b2w)

    ix, iy = lax.axis_index("gx"), lax.axis_index("gy")
    at_x = {a: lax.rem(ix + (a + gx_size), gx_size) for a in range(-4, 5)}
    at_y = {a: lax.rem(iy + (a + gy_size), gy_size) for a in range(-4, 5)}

    def device(a, c):
        return {"gx": at_x[a], "gy": at_y[c]}

    def send(name):
        level, colours, msgs = GROUPS[name]
        k, n = NAMES.index(name), N[level]
        for a, c, x0, nx, y0, ny in msgs:
            here = (pl.ds(HX[level] + x0 + a * n, nx), pl.ds(HY[level] + y0 + c * n, ny))
            there = (pl.ds(HX[level] + x0, nx), pl.ds(HY[level] + y0, ny))
            if colours == 2:
                here, there = (slice(None),) + here, (slice(None),) + there
            pltpu.make_async_remote_copy(
                src_ref=sent[name].at[here], dst_ref=landed[name].at[there],
                send_sem=send_sem.at[k], recv_sem=recv_sem.at[k],
                device_id=device(a, c), device_id_type=MESH,
            ).start()

    def await_bytes(sem, name):
        block = dummy.at[pl.ds(0, COUNT[name])]
        pltpu.make_async_copy(block, block, sem.at[NAMES.index(name)]).wait()

    def receive(*names):
        for name in names:
            await_bytes(recv_sem, name)

    lane = lax.broadcasted_iota(jnp.int32, (8, LANES), 1)
    odd8 = odd_rows(8, 0)

    def weights(kind):
        down = jnp.logical_not(odd8) if kind == 0 else odd8
        first = jnp.where(jnp.logical_and(down, lane > 0), 1.0, 0.0)
        second = jnp.where(jnp.logical_and(jnp.logical_not(down), lane < LANES - 1), 1.0, 0.0)
        return first[None], second[None], (1.0 - first - second)[None]

    weight = (weights(0), weights(1))

    def load(ref, lead, y0, n):
        return ref[lead + (pl.ds(y0, n),)].reshape(n // 8, 8, LANES)

    def store(ref, lead, y0, n, value):
        ref[lead + (pl.ds(y0, n),)] = value.reshape(n, LANES)

    def beside(same, kind):
        flat = same.reshape(-1, LANES)
        lower = pltpu.roll(flat, 1, 1).reshape(same.shape)
        upper = pltpu.roll(flat, LANES - 1, 1).reshape(same.shape)
        return lower * weight[kind][0] + upper * weight[kind][1]

    def around(ref, other, x, y0, n):
        return (load(ref, (other, x - 1), y0, n) + load(ref, (other, x + 1), y0, n)) + (
            load(ref, (other, x), y0 - 1, n) + load(ref, (other, x), y0 + 1, n))

    def set_up(level, x0, nx, y0, n):
        wh = WH[level]

        def body(x, px):
            for c in (0, 1):
                kind = (c + px) % 2
                centre = load(beta[level], (c, x), y0, n)
                same = load(beta[level], (1 - c, x), y0, n)
                vertical = same + beside(same, kind) + centre * weight[kind][2]
                total = centre * (4 * wh + 2 * WV) + wh * around(beta[level], 1 - c, x, y0, n) + WV * vertical
                store(inv[level], (c, x), y0, n, 1.0 / total)
                if c == 0 and level < 3:
                    store(diag[level], (x,), y0, n, total)

        rows(x0, nx, body, 2)

    def coupled(level, c, x, px, y0, n):
        wh, kind = WH[level], (c + px) % 2
        same_p, same_q = load(p[level], (1 - c, x), y0, n), load(q[level], (1 - c, x), y0, n)
        sum_p = wh * around(p[level], 1 - c, x, y0, n) + WV * (same_p + beside(same_p, kind))
        sum_q = wh * around(q[level], 1 - c, x, y0, n) + WV * (same_q + beside(same_q, kind))
        centre = load(beta[level], (c, x), y0, n)
        return centre, centre * sum_p + sum_q

    def half_sweep(level, c, radius, y0, n, rhs=None):
        rhs = b[level] if rhs is None else rhs

        def body(x, px):
            centre, total = coupled(level, c, x, px, y0, n)
            value = (load(rhs, (c, x), y0, n) + total) * load(inv[level], (c, x), y0, n)
            store(p[level], (c, x), y0, n, value)
            store(q[level], (c, x), y0, n, centre * value)

        rows(HX[level] - radius, N[level] + 2 * radius, body)

    def first_half(level, radius, y0, n):
        def body(x, px):
            value = load(b[level], (0, x), y0, n) * load(inv[level], (0, x), y0, n)
            store(p[level], (0, x), y0, n, value)
            store(q[level], (0, x), y0, n, load(beta[level], (0, x), y0, n) * value)

        rows(HX[level] - radius, N[level] + 2 * radius, body)

    def put_coarse(ref, level, i, even, odd):
        n = N[level]

        def put(parity):
            swapped = odd_rows(n, parity)
            here = (HX[level] + i, pl.ds(HY[level], n))
            ref[(0,) + here] = jnp.where(swapped, odd, even)
            ref[(1,) + here] = jnp.where(swapped, even, odd)

        return put

    def coarsen_beta(level):
        n = N[level + 1]

        def body(i, pi):
            def child(c, a, k):
                return beta[level][c, HX[level] + 2 * i + a, pl.ds(HY[level] + k, n, stride=2), :]

            even = 0.25 * ((child(0, 0, 0) + child(0, 1, 1)) + (child(1, 0, 1) + child(1, 1, 0)))
            odd = 0.25 * ((child(1, 0, 0) + child(1, 1, 1)) + (child(0, 0, 1) + child(0, 1, 0)))
            put_coarse(beta[level + 1], level + 1, i, even, odd)(pi)

        rows(0, n, body)

    def residual(level):
        n, nc = N[level], N[level + 1]
        padded = max(8, n)

        def body(x, px):
            _, total = coupled(level, 0, x, px, HY[level], padded)
            left = load(b[level], (0, x), HY[level], padded) + total
            left = left - load(diag[level], (x,), HY[level], padded) * load(p[level], (0, x), HY[level], padded)
            store(res, (x - HX[level],), 0, padded, left)
            field[level][x, pl.ds(HY[level], n)] = p[level][1, x, pl.ds(HY[level], n)]

        rows(HX[level], n, body)

        def restrict(i, pi):
            def child(a, k):
                return res[2 * i + a, pl.ds(k, nc, stride=2), :]

            put_coarse(b[level + 1], level + 1, i, 0.25 * (child(0, 0) + child(1, 1)), 0.25 * (child(0, 1) + child(1, 0)))(pi)

        rows(0, nc, restrict)

    def prolong(level, x0, nx, y0, n):
        half = n // 2
        i0 = HX[level + 1] + (x0 - HX[level]) // 2
        j0 = HY[level + 1] + (y0 - HY[level]) // 2

        def body(i, pi):
            red = p[level + 1][0, i, pl.ds(j0, half), :]
            black = p[level + 1][1, i, pl.ds(j0, half), :]
            swapped = odd_rows(half, j0 + pi)
            even, odd = jnp.where(swapped, black, red), jnp.where(swapped, red, black)
            for a in (0, 1):
                x = x0 + 2 * (i - i0) + a
                for k in (0, 1):
                    here = (pl.ds(y0 + k, half, stride=2), slice(None))
                    value = field[level][(x,) + here] + (odd if a == k else even)
                    p[level][(1, x) + here] = value
                    q[level][(1, x) + here] = beta[level][(1, x) + here] * value

        rows(i0, nx // 2, body, 2)

    def descend(level, y0, n):
        first_half(level, 4, y0, n)
        half_sweep(level, 1, 3, y0, n)
        half_sweep(level, 0, 2, y0, n)
        half_sweep(level, 1, 1, y0, n)
        residual(level)

    barrier = pltpu.get_barrier_semaphore()
    for a, c in PARTNERS:
        pl.semaphore_signal(barrier, inc=1, device_id=device(a, c), device_id_type=MESH)

    wide = lax.broadcasted_iota(jnp.int32, (16, LANES), 1)

    def take(x, px):
        odd = odd_rows(16, px).astype(jnp.int32)
        low = wide < LANES // 2
        for ref, to in ((inv_ref, e0), (src_ref, b0)):
            lower, upper = ref[x, :, pl.ds(0, LANES)], ref[x, :, pl.ds(LANES, LANES)]
            for c in (0, 1):
                slot = lax.rem(2 * wide + (odd if c == 0 else 1 - odd), LANES)
                value = jnp.where(low, jnp.take_along_axis(lower, slot, axis=1), jnp.take_along_axis(upper, slot, axis=1))
                to[c, HX[0] + x, pl.ds(HY[0], 16)] = value

    rows(0, 16, take)
    pl.semaphore_wait(barrier, len(PARTNERS))
    send("e0")
    send("b0")
    for level in (0, 1, 2):
        coarsen_beta(level)
    send("e1")
    receive("e0")
    receive("b0")
    set_up(0, 2, 24, 2, 24)
    descend(0, 2, 24)

    send("b1")
    send("f0")
    send("e2")
    receive("e1")
    set_up(1, 2, 20, 2, 24)
    receive("b1")
    descend(1, 6, 16)

    send("b2")
    send("f1")
    send("e3")
    receive("e2")
    set_up(2, 1, 18, 2, 24)
    receive("b2")
    descend(2, 6, 16)

    send("b3")
    send("b2far")
    send("f2")
    receive("e3")
    set_up(3, 2, 14, 2, 16)
    receive("b3")
    first_half(3, 6, 2, 16)
    for step in range(1, 7):
        half_sweep(3, step % 2, 6 - step, 2, 16)
    for x in range(HX[3], HX[3] + N[3]):
        f3[x, pl.ds(HY[3], N[3])] = p3[0, x, pl.ds(HY[3], N[3])]
    send("f3")

    def keep_rhs(x, px):
        for c in (0, 1):
            b2w[c, x, pl.ds(6, 12)] = b2[c, x, pl.ds(6, 12)]

    rows(4, 12, keep_rhs)
    for name in NAMES:
        if name != "f3":
            await_bytes(send_sem, name)
    receive("f3")

    def red_back(x, px):
        value = load(f3, (x,), 2, 16)
        store(p3, (0, x), 2, 16, value)
        store(q3, (0, x), 2, 16, load(e3, (0, x), 2, 16) * value)

    rows(2, 14, red_back)
    half_sweep(3, 1, 5, 2, 16)

    receive("b2far")
    receive("f2")
    prolong(2, 0, 20, 2, 24)
    for step in range(4):
        half_sweep(2, step % 2, 7 - step, 2, 24, b2w)
    receive("f1")
    prolong(1, 0, 24, 2, 24)
    for step in range(4):
        half_sweep(1, step % 2, 6 - step, 2, 24)
    receive("f0")
    prolong(0, 2, 24, 2, 24)
    half_sweep(0, 0, 3, 2, 24)
    half_sweep(0, 1, 2, 2, 24)
    half_sweep(0, 0, 1, 2, 24)
    half_sweep(0, 1, 0, 6, 16)

    def give(x, px):
        red, black = p0[0, HX[0] + x, pl.ds(HY[0], 16)], p0[1, HX[0] + x, pl.ds(HY[0], 16)]
        is_red = (wide + odd_rows(16, px).astype(jnp.int32)) % 2 == 0
        for part in (0, 1):
            slot = wide // 2 + part * (LANES // 2)
            out_ref[x, :, pl.ds(part * LANES, LANES)] = jnp.where(
                is_red, jnp.take_along_axis(red, slot, axis=1), jnp.take_along_axis(black, slot, axis=1))

    rows(0, 16, give)
    await_bytes(send_sem, "f3")


def solution(mesh):
    gx_size, gy_size = mesh.shape["gx"], mesh.shape["gy"]

    def both(level):
        return pltpu.VMEM((2, XE[level], YE[level], LANES), jnp.float32)

    def single(level):
        return pltpu.VMEM((XE[level], YE[level], LANES), jnp.float32)

    levels = range(4)
    scratch = [both(level) for _ in range(5) for level in levels]
    scratch += [single(level) for level in range(3)] + [single(level) for level in levels]
    scratch += [both(2), pltpu.VMEM((16, 16, LANES), jnp.float32), pltpu.VMEM((MOST, LANES), jnp.float32)]
    scratch += [pltpu.SemaphoreType.DMA((len(NAMES),))] * 2

    def on_device(source, inv_density):
        vmem = pl.BlockSpec(memory_space=pltpu.VMEM)

        def body(*refs):
            kernel(gx_size, gy_size, *refs)

        return pl.pallas_call(
            body,
            out_shape=jax.ShapeDtypeStruct(source.shape, jnp.float32),
            in_specs=[vmem, vmem],
            out_specs=vmem,
            scratch_shapes=scratch,
            name="v_cycle",
            compiler_params=pltpu.CompilerParams(
                collective_id=0, has_side_effects=True, vmem_limit_bytes=40 << 20
            ),
        )(source, inv_density)

    placed = P("gx", "gy", None)
    return jax.shard_map(
        on_device, mesh=mesh, in_specs=(placed, placed), out_specs=placed, check_vma=False
    )
```

```python
import jax
import jax.numpy as jnp
from jax import lax
from jax.experimental import pallas as pl
from jax.experimental.pallas import tpu as pltpu
from jax.sharding import PartitionSpec as P


MESH = pl.DeviceIdType.MESH
N = (16, 8, 4, 2)
HX = (6, 8, 8, 8)
HY = (6, 10, 10, 8)
XE = (28, 24, 20, 18)
YE = (32, 32, 32, 24)
WH = (0.5, 0.125, 0.03125, 0.0078125)
WV = 0.125
LANES = 128
GROUP = 24


def spread(n, radius, keep=None):
    out = []
    reach = -(-radius // n)
    for a in range(-reach, reach + 1):
        for b in range(-reach, reach + 1):
            gap_x = (abs(a) - 1) * n + 1 if a else 0
            gap_y = (abs(b) - 1) * n + 1 if b else 0
            if (a, b) == (0, 0) or gap_x + gap_y > radius:
                continue
            if keep is not None and not keep(a, b):
                continue
            rx, ry = radius - gap_y, radius - gap_x
            x0, x1 = max(-a * n, -rx), min(-a * n + n, n + rx)
            y0, y1 = max(-b * n, -ry), min(-b * n + n, n + ry)
            out.append((a, b, x0, x1 - x0, y0, y1 - y0))
    return sorted(out, key=lambda m: (m[1] != 0, m[0] == 0))


def near(a, b):
    return max(abs(a), abs(b)) == 1


def far(a, b):
    return max(abs(a), abs(b)) > 1


BOTH, ONE, RED, BLACK = (slice(None),), (), (0,), (1,)
GROUPS = {
    "b0": (0, RED, spread(16, 4)),
    "b0k": (0, BLACK, spread(16, 3)),
    "e0": (0, RED, spread(16, 4)),
    "e0k": (0, BLACK, spread(16, 5)),
    "e1": (1, BOTH, spread(8, 7)),
    "e2": (2, BOTH, spread(4, 8)),
    "e3": (3, BOTH, spread(2, 7)),
    "f0": (0, ONE, spread(16, 4)),
    "b1": (1, BOTH, spread(8, 6)),
    "f1": (1, ONE, spread(8, 7)),
    "b2": (2, BOTH, spread(4, 8, near)),
    "b2far": (2, BOTH, spread(4, 7, far)),
    "f2": (2, ONE, spread(4, 8)),
    "b3": (3, BOTH, spread(2, 6)),
    "f3": (3, ONE, spread(2, 6)),
}
NAMES = tuple(GROUPS)
COUNT = {k: (2 if c == BOTH else 1) * sum(m[3] * m[5] for m in msgs) for k, (_, c, msgs) in GROUPS.items()}
MOST = -(-max(COUNT.values()) // 8) * 8
PARTNERS = [m[:2] for m in GROUPS["e2"][2]]


def rows(x0, nx, body, group=4):
    steps = nx // group
    if steps > 1:

        def step(i, carry):
            for j in range(group):
                body(x0 + i * group + j, (x0 + j) % 2)
            return carry

        lax.fori_loop(0, steps, step, 0)
        done = steps * group
    else:
        done = 0
    for j in range(done, nx):
        body(x0 + j, (x0 + j) % 2)


def odd_rows(n, offset):
    return (lax.broadcasted_iota(jnp.int32, (n, LANES), 0) + offset) % 2 == 1


def lines(level, radius):
    return HY[level] - radius, -(-(N[level] + 2 * radius) // 8) * 8


def kernel(gx_size, gy_size, src_hbm, inv_hbm, out_ref, *scratch):
    beta, b, norm, red_p, black_p, coef = (scratch[4 * k : 4 * k + 4] for k in range(6))
    diag, field = scratch[24:27], scratch[27:31]
    b2w, res, src_ref, inv_ref, dummy, load_sem, send_sem, recv_sem = scratch[31:]
    sent = {"b2far": b[2], "b0k": b[0], "e0k": beta[0]}
    for level in range(4):
        sent.update({"e%d" % level: beta[level], "b%d" % level: b[level], "f%d" % level: field[level]})
    landed = dict(sent, b2far=b2w)

    ix, iy = lax.axis_index("gx"), lax.axis_index("gy")
    at_x = {a: lax.rem(ix + (a + gx_size), gx_size) for a in range(-4, 5)}
    at_y = {a: lax.rem(iy + (a + gy_size), gy_size) for a in range(-4, 5)}

    def device(a, c):
        return {"gx": at_x[a], "gy": at_y[c]}

    def send(name):
        level, colours, msgs = GROUPS[name]
        k, n = NAMES.index(name), N[level]
        for a, c, x0, nx, y0, ny in msgs:
            here = (pl.ds(HX[level] + x0 + a * n, nx), pl.ds(HY[level] + y0 + c * n, ny))
            there = (pl.ds(HX[level] + x0, nx), pl.ds(HY[level] + y0, ny))
            here, there = colours + here, colours + there
            pltpu.make_async_remote_copy(
                src_ref=sent[name].at[here], dst_ref=landed[name].at[there],
                send_sem=send_sem.at[k], recv_sem=recv_sem.at[k],
                device_id=device(a, c), device_id_type=MESH,
            ).start()

    def await_bytes(sem, name):
        block = dummy.at[pl.ds(0, COUNT[name])]
        pltpu.make_async_copy(block, block, sem.at[NAMES.index(name)]).wait()

    def receive(*names):
        for name in names:
            await_bytes(recv_sem, name)

    lane = lax.broadcasted_iota(jnp.int32, (8, LANES), 1)
    odd8 = odd_rows(8, 0)

    def weights(kind):
        down = jnp.logical_not(odd8) if kind == 0 else odd8
        has = jnp.where(down, jnp.where(lane > 0, 1.0, 0.0), jnp.where(lane < LANES - 1, 1.0, 0.0))
        return jnp.where(down, 1.0, 0.0)[None], has[None]

    weight = (weights(0), weights(1))

    def load(ref, lead, y0, n):
        return ref[lead + (pl.ds(y0, n),)].reshape(n // 8, 8, LANES)

    def store(ref, lead, y0, n, value):
        ref[lead + (pl.ds(y0, n),)] = value.reshape(n, LANES)

    def beside(same, kind):
        flat = same.reshape(-1, LANES)
        lower = pltpu.roll(flat, 1, 1).reshape(same.shape)
        upper = pltpu.roll(flat, LANES - 1, 1).reshape(same.shape)
        return jnp.where(weight[kind][0] > 0.0, lower, upper)

    def set_up(level, radius, group):
        wh = WH[level]
        y0, n = lines(level, radius)

        def body(x, px):
            for c in (0, 1):
                kind = (c + px + y0) % 2
                at = lambda dx, dy: load(beta[level], (1 - c, x + dx), y0 + dy, n)
                centre, same = load(beta[level], (c, x), y0, n), at(0, 0)
                has = weight[kind][1]
                other = beside(same, kind)
                other = other * has + centre * (1.0 - has)
                sides = (at(1, 0), at(-1, 0), at(0, 1), at(0, -1))
                total = centre * (4 * wh + 2 * WV) + wh * ((sides[0] + sides[1]) + (sides[2] + sides[3])) + WV * (same + other)
                inverse = 1.0 / total
                across, upright = wh * inverse, WV * inverse
                for k, side in enumerate(sides):
                    store(coef[level], (k, c, x), y0, n, (centre + side) * across)
                store(coef[level], (4, c, x), y0, n, (centre + same) * upright)
                store(coef[level], (5, c, x), y0, n, (centre + other) * (upright * has))
                store(coef[level], (6, c, x), y0, n, inverse)
                if c == 0 and level < 3:
                    store(diag[level], (x,), y0, n, total)

        rows(HX[level] - radius, N[level] + 2 * radius, body, group)

    def normalise(level, radius, rhs=None):
        y0, n = lines(level, radius)
        rhs = b[level] if rhs is None else rhs

        def body(x, px):
            for c in (0, 1):
                store(norm[level], (c, x), y0, n, load(rhs, (c, x), y0, n) * load(coef[level], (6, c, x), y0, n))

        rows(HX[level] - radius, N[level] + 2 * radius, body, 10)

    def solved(level, c, x0, count, y0, n, other, lead=()):
        mids = [load(other, lead + (x0 + j - 1,), y0, n) for j in range(count + 2)]
        out = []
        for j in range(count):
            x = x0 + j
            kind = (c + j + y0) % 2
            factor = lambda k: load(coef[level], (k, c, x), y0, n)
            value = load(norm[level], (c, x), y0, n) + mids[j + 2] * factor(0)
            value2 = mids[j] * factor(1) + load(other, lead + (x,), y0 + 1, n) * factor(2)
            value3 = load(other, lead + (x,), y0 - 1, n) * factor(3) + mids[j + 1] * factor(4)
            out.append((kind, mids[j + 1], factor(5), (value + value2) + value3))
        return out

    def finish(out, px):
        return [total + beside(same, (kind + px) % 2) * factor for kind, same, factor, total in out]

    def chunks(x0, count, body, group):
        steps = count // group
        if steps > 1:

            def step(i, carry):
                body(x0 + i * group, x0 % 2, group)
                return carry

            lax.fori_loop(0, steps, step, 0)
            left = count - steps * group
        else:
            left = count
        if left:
            body(x0 + count - left, (x0 + count - left) % 2, left)

    def half_sweep(level, c, radius, other=None, lead=(), group=GROUP):
        y0, n = lines(level, radius)
        mine = (red_p, black_p)[c][level]
        other = (black_p, red_p)[c][level] if other is None else other

        def body(x, px, count):
            values = finish(solved(level, c, x, count, y0, n, other, lead), px)
            for j, value in enumerate(values):
                store(mine, (x + j,), y0, n, value)

        chunks(HX[level] - radius, N[level] + 2 * radius, body, group)

    def put_coarse(ref, level, i, even, odd):
        n = N[level]

        def put(parity):
            swapped = odd_rows(n, parity)
            here = (HX[level] + i, pl.ds(HY[level], n))
            ref[(0,) + here] = jnp.where(swapped, odd, even)
            ref[(1,) + here] = jnp.where(swapped, even, odd)

        return put

    def coarsen_beta(level):
        n = N[level + 1]

        def body(i, pi):
            def child(c, a, k):
                return beta[level][c, HX[level] + 2 * i + a, pl.ds(HY[level] + k, n, stride=2), :]

            even = 0.25 * ((child(0, 0, 0) + child(0, 1, 1)) + (child(1, 0, 1) + child(1, 1, 0)))
            odd = 0.25 * ((child(1, 0, 0) + child(1, 1, 1)) + (child(0, 0, 1) + child(0, 1, 0)))
            put_coarse(beta[level + 1], level + 1, i, even, odd)(pi)

        rows(0, n, body)

    def residual(level):
        n, nc = N[level], N[level + 1]
        y0, padded = lines(level, 0)

        def body(x, px, count):
            values = finish(solved(level, 0, x, count, y0, padded, black_p[level]), px)
            for j, value in enumerate(values):
                left = (value - load(red_p[level], (x + j,), y0, padded)) * load(diag[level], (x + j,), y0, padded)
                store(res, (x + j - HX[level],), 0, padded, left)
                field[level][x + j, pl.ds(y0, n)] = black_p[level][x + j, pl.ds(y0, n)]

        chunks(HX[level], n, body, GROUP)

        def restrict(i, pi):
            def child(a, k):
                return res[2 * i + a, pl.ds(k, nc, stride=2), :]

            put_coarse(b[level + 1], level + 1, i, 0.25 * (child(0, 0) + child(1, 1)), 0.25 * (child(0, 1) + child(1, 0)))(pi)

        rows(0, nc, restrict, 8)

    def prolong(level, x0, nx, y0, n, red):
        half = n // 2
        i0 = HX[level + 1] + (x0 - HX[level]) // 2
        j0 = HY[level + 1] + (y0 - HY[level]) // 2

        def body(i, pi):
            first, second = red[i, pl.ds(j0, half), :], black_p[level + 1][i, pl.ds(j0, half), :]
            swapped = odd_rows(half, j0 + pi)
            even, odd = jnp.where(swapped, second, first), jnp.where(swapped, first, second)
            for a in (0, 1):
                x = x0 + 2 * (i - i0) + a
                for k in (0, 1):
                    here = (x, pl.ds(y0 + k, half, stride=2), slice(None))
                    black_p[level][here] = field[level][here] + (odd if a == k else even)

        rows(i0, nx // 2, body, 6)

    def descend(level):
        half_sweep(level, 1, 3, norm[level], (0,))
        half_sweep(level, 0, 2)
        half_sweep(level, 1, 1)
        residual(level)

    barrier = pltpu.get_barrier_semaphore()
    for a, c in PARTNERS:
        pl.semaphore_signal(barrier, inc=1, device_id=device(a, c), device_id_type=MESH)
    fetch_inv = pltpu.make_async_copy(inv_hbm, inv_ref, load_sem.at[0])
    fetch_src = pltpu.make_async_copy(src_hbm, src_ref, load_sem.at[1])
    fetch_inv.start()
    fetch_src.start()

    wide = lax.broadcasted_iota(jnp.int32, (16, LANES), 1)

    def take(ref, to):
        def body(x, px):
            odd = odd_rows(16, px).astype(jnp.int32)
            low = wide < LANES // 2
            lower, upper = ref[x, :, pl.ds(0, LANES)], ref[x, :, pl.ds(LANES, LANES)]
            for c in (0, 1):
                slot = lax.rem(2 * wide + (odd if c == 0 else 1 - odd), LANES)
                value = jnp.where(low, jnp.take_along_axis(lower, slot, axis=1), jnp.take_along_axis(upper, slot, axis=1))
                to[c, HX[0] + x, pl.ds(HY[0], 16)] = value

        rows(0, 16, body, 8)

    fetch_inv.wait()
    take(inv_ref, beta[0])
    pl.semaphore_wait(barrier, len(PARTNERS))
    send("e0k")
    send("e0")
    fetch_src.wait()
    take(src_ref, b[0])
    send("b0")
    send("b0k")
    for level in (0, 1, 2):
        coarsen_beta(level)
    send("e1")
    send("e2")
    receive("e0k", "e0", "b0", "b0k")
    set_up(0, 4, 8)
    normalise(0, 4)
    descend(0)

    send("b1")
    receive("e1")
    set_up(1, 6, 4)
    receive("b1")
    normalise(1, 6)
    descend(1)

    send("b2")
    send("e3")
    receive("e2")
    set_up(2, 7, 6)
    receive("b2")
    normalise(2, 4)
    descend(2)

    send("b3")
    send("b2far")
    send("f2")
    receive("e3")
    set_up(3, 6, 14)
    receive("b3")
    normalise(3, 6)
    half_sweep(3, 1, 5, norm[3], (0,))
    for step in range(2, 7):
        half_sweep(3, step % 2, 6 - step)
    for x in range(HX[3], HX[3] + N[3]):
        field[3][x, pl.ds(HY[3], N[3])] = red_p[3][x, pl.ds(HY[3], N[3])]
    send("f3")
    send("f1")
    send("f0")

    def keep_rhs(x, px):
        for c in (0, 1):
            b2w[c, x, pl.ds(6, 12)] = b[2][c, x, pl.ds(6, 12)]

    rows(4, 12, keep_rhs, 6)
    for name in NAMES:
        if name not in ("f0", "f1", "f3"):
            await_bytes(send_sem, name)
    receive("b2far")
    normalise(2, 7, b2w)
    receive("f2")
    receive("f3")
    half_sweep(3, 1, 5, field[3])

    prolong(2, 0, 20, 2, 24, field[3])
    for step in range(4):
        half_sweep(2, step % 2, 7 - step)
    receive("f1")
    prolong(1, 0, 24, 2, 24, red_p[2])
    for step in range(4):
        half_sweep(1, step % 2, 6 - step)
    receive("f0")
    prolong(0, 2, 24, 2, 24, red_p[1])
    for step in range(4):
        half_sweep(0, step % 2, 3 - step)

    def give(x, px):
        red, black = red_p[0][HX[0] + x, pl.ds(HY[0], 16)], black_p[0][HX[0] + x, pl.ds(HY[0], 16)]
        is_red = (wide + odd_rows(16, px).astype(jnp.int32)) % 2 == 0
        for part in (0, 1):
            slot = wide // 2 + part * (LANES // 2)
            out_ref[x, :, pl.ds(part * LANES, LANES)] = jnp.where(
                is_red, jnp.take_along_axis(red, slot, axis=1), jnp.take_along_axis(black, slot, axis=1))

    rows(0, 16, give, 8)
    for name in ("f0", "f1", "f3"):
        await_bytes(send_sem, name)


def solution(mesh):
    gx_size, gy_size = mesh.shape["gx"], mesh.shape["gy"]

    def both(level):
        return pltpu.VMEM((2, XE[level], YE[level], LANES), jnp.float32)

    def single(level):
        return pltpu.VMEM((XE[level], YE[level], LANES), jnp.float32)

    levels = range(4)
    block = pltpu.VMEM((16, 16, 2 * LANES), jnp.float32)
    scratch = [both(level) for _ in range(3) for level in levels]
    scratch += [single(level) for _ in range(2) for level in levels]
    scratch += [pltpu.VMEM((7, 2, XE[level], YE[level], LANES), jnp.float32) for level in levels]
    scratch += [single(level) for level in range(3)] + [single(level) for level in levels]
    scratch += [both(2), pltpu.VMEM((16, 16, LANES), jnp.float32), block, block]
    scratch += [pltpu.VMEM((MOST, LANES), jnp.float32), pltpu.SemaphoreType.DMA((2,))]
    scratch += [pltpu.SemaphoreType.DMA((len(NAMES),))] * 2

    def on_device(source, inv_density):
        hbm = pl.BlockSpec(memory_space=pltpu.HBM)

        def body(*refs):
            kernel(gx_size, gy_size, *refs)

        return pl.pallas_call(
            body,
            out_shape=pltpu.VMEM(source.shape, jnp.float32),
            in_specs=[hbm, hbm],
            out_specs=pl.BlockSpec(memory_space=pltpu.VMEM),
            scratch_shapes=scratch,
            name="v_cycle",
            compiler_params=pltpu.CompilerParams(
                collective_id=0, has_side_effects=True, vmem_limit_bytes=60 << 20
            ),
        )(source, inv_density)

    placed = P("gx", "gy", None)
    return jax.shard_map(
        on_device, mesh=mesh, in_specs=(placed, placed), out_specs=placed, check_vma=False
    )
```

```python
import jax
import jax.numpy as jnp
from jax import lax
from jax.experimental import pallas as pl
from jax.experimental.pallas import tpu as pltpu
from jax.sharding import PartitionSpec as P


MESH = pl.DeviceIdType.MESH
N = (16, 8, 4, 2)
HX = (6, 8, 8, 8)
HY = (6, 10, 10, 8)
XE = (28, 24, 20, 18)
YE = (32, 32, 32, 24)
WH = (0.5, 0.125, 0.03125, 0.0078125)
WV = 0.125
LANES = 128
GROUP = 24


def spread(n, radius, keep=None):
    out = []
    reach = -(-radius // n)
    for a in range(-reach, reach + 1):
        for b in range(-reach, reach + 1):
            gap_x = (abs(a) - 1) * n + 1 if a else 0
            gap_y = (abs(b) - 1) * n + 1 if b else 0
            if (a, b) == (0, 0) or gap_x + gap_y > radius:
                continue
            if keep is not None and not keep(a, b):
                continue
            rx, ry = radius - gap_y, radius - gap_x
            x0, x1 = max(-a * n, -rx), min(-a * n + n, n + rx)
            y0, y1 = max(-b * n, -ry), min(-b * n + n, n + ry)
            out.append((a, b, x0, x1 - x0, y0, y1 - y0))
    return sorted(out, key=lambda m: (m[1] != 0, m[0] == 0))


def along_x(n, radius):
    return [m for m in spread(n, radius) if m[1] == 0]


def along_y(n, radius):
    out = []
    for _, c, _, _, y0, ny in [m for m in spread(n, radius) if m[0] == 0]:
        width = radius - ((abs(c) - 1) * n + 1)
        out.append((0, c, -width, n + 2 * width, y0, ny))
    return out


def near(a, b):
    return max(abs(a), abs(b)) == 1


def far(a, b):
    return max(abs(a), abs(b)) > 1


BOTH, ONE, RED, BLACK = (slice(None),), (), (0,), (1,)
GROUPS = {
    "b0": (0, RED, spread(16, 4)),
    "b0k": (0, BLACK, spread(16, 3)),
    "e0": (0, RED, spread(16, 4)),
    "e0k": (0, BLACK, spread(16, 5)),
    "e1": (1, BOTH, spread(8, 7)),
    "e2x": (2, BOTH, along_x(4, 8)),
    "e2y": (2, BOTH, along_y(4, 8)),
    "e3x": (3, BOTH, along_x(2, 7)),
    "e3y": (3, BOTH, along_y(2, 7)),
    "f0x": (0, ONE, along_x(16, 4)),
    "f0y": (0, ONE, along_y(16, 4)),
    "b1": (1, BOTH, spread(8, 6)),
    "f1x": (1, ONE, along_x(8, 7)),
    "f1y": (1, ONE, along_y(8, 7)),
    "b2": (2, BOTH, spread(4, 8, near)),
    "b2far": (2, BOTH, spread(4, 7, far)),
    "f2x": (2, ONE, along_x(4, 8)),
    "f2y": (2, ONE, along_y(4, 8)),
    "b3": (3, BOTH, spread(2, 6)),
    "f3": (3, ONE, spread(2, 6)),
}
NAMES = tuple(GROUPS)
COUNT = {k: (2 if c == BOTH else 1) * sum(m[3] * m[5] for m in msgs) for k, (_, c, msgs) in GROUPS.items()}
MOST = -(-max(COUNT.values()) // 8) * 8
PARTNERS = [m[:2] for m in spread(1, 2, near)] + [(a, 0) for a in (-4, -3, -2, 2, 3, 4)] + [(0, -4), (0, 4)]


def rows(x0, nx, body, group=4):
    steps = nx // group
    if steps > 1:

        def step(i, carry):
            for j in range(group):
                body(x0 + i * group + j, (x0 + j) % 2)
            return carry

        lax.fori_loop(0, steps, step, 0)
        done = steps * group
    else:
        done = 0
    for j in range(done, nx):
        body(x0 + j, (x0 + j) % 2)


def odd_rows(n, offset):
    return (lax.broadcasted_iota(jnp.int32, (n, LANES), 0) + offset) % 2 == 1


def lines(level, radius):
    return HY[level] - radius, -(-(N[level] + 2 * radius) // 8) * 8


def kernel(gx_size, gy_size, src_hbm, inv_hbm, out_ref, *scratch):
    beta, b, norm, red_p, black_p, coef = (scratch[4 * k : 4 * k + 4] for k in range(6))
    diag, field = scratch[24:27], scratch[27:31]
    b2w, res, src_ref, inv_ref, dummy, load_sem, send_sem, recv_sem = scratch[31:]
    sent = {"b2far": b[2], "b0k": b[0], "e0k": beta[0]}
    for level in range(4):
        for end in ("", "x", "y"):
            sent.update({"e%d%s" % (level, end): beta[level], "f%d%s" % (level, end): field[level]})
        sent["b%d" % level] = b[level]
    landed = dict(sent, b2far=b2w)

    ix, iy = lax.axis_index("gx"), lax.axis_index("gy")
    at_x = {a: lax.rem(ix + (a + gx_size), gx_size) for a in range(-4, 5)}
    at_y = {a: lax.rem(iy + (a + gy_size), gy_size) for a in range(-4, 5)}

    def device(a, c):
        return {"gx": at_x[a], "gy": at_y[c]}

    def send(name):
        level, colours, msgs = GROUPS[name]
        k, n = NAMES.index(name), N[level]
        for a, c, x0, nx, y0, ny in msgs:
            here = (pl.ds(HX[level] + x0 + a * n, nx), pl.ds(HY[level] + y0 + c * n, ny))
            there = (pl.ds(HX[level] + x0, nx), pl.ds(HY[level] + y0, ny))
            here, there = colours + here, colours + there
            pltpu.make_async_remote_copy(
                src_ref=sent[name].at[here], dst_ref=landed[name].at[there],
                send_sem=send_sem.at[k], recv_sem=recv_sem.at[k],
                device_id=device(a, c), device_id_type=MESH,
            ).start()

    def await_bytes(sem, name):
        block = dummy.at[pl.ds(0, COUNT[name])]
        pltpu.make_async_copy(block, block, sem.at[NAMES.index(name)]).wait()

    def receive(*names):
        for name in names:
            await_bytes(recv_sem, name)

    lane = lax.broadcasted_iota(jnp.int32, (8, LANES), 1)
    odd8 = odd_rows(8, 0)

    def weights(kind):
        down = jnp.logical_not(odd8) if kind == 0 else odd8
        has = jnp.where(down, jnp.where(lane > 0, 1.0, 0.0), jnp.where(lane < LANES - 1, 1.0, 0.0))
        return jnp.where(down, 1.0, 0.0)[None], has[None]

    weight = (weights(0), weights(1))

    def load(ref, lead, y0, n):
        return ref[lead + (pl.ds(y0, n),)].reshape(n // 8, 8, LANES)

    def store(ref, lead, y0, n, value):
        ref[lead + (pl.ds(y0, n),)] = value.reshape(n, LANES)

    def beside(same, kind):
        flat = same.reshape(-1, LANES)
        lower = pltpu.roll(flat, 1, 1).reshape(same.shape)
        upper = pltpu.roll(flat, LANES - 1, 1).reshape(same.shape)
        return jnp.where(weight[kind][0] > 0.0, lower, upper)

    def set_up(level, radius, group):
        wh = WH[level]
        y0, n = lines(level, radius)

        def body(x, px):
            for c in (0, 1):
                kind = (c + px + y0) % 2
                at = lambda dx, dy: load(beta[level], (1 - c, x + dx), y0 + dy, n)
                centre, same = load(beta[level], (c, x), y0, n), at(0, 0)
                has = weight[kind][1]
                other = beside(same, kind)
                other = other * has + centre * (1.0 - has)
                sides = (at(1, 0), at(-1, 0), at(0, 1), at(0, -1))
                total = centre * (4 * wh + 2 * WV) + wh * ((sides[0] + sides[1]) + (sides[2] + sides[3])) + WV * (same + other)
                inverse = 1.0 / total
                across, upright = wh * inverse, WV * inverse
                for k, side in enumerate(sides):
                    store(coef[level], (k, c, x), y0, n, (centre + side) * across)
                store(coef[level], (4, c, x), y0, n, (centre + same) * upright)
                store(coef[level], (5, c, x), y0, n, (centre + other) * (upright * has))
                store(coef[level], (6, c, x), y0, n, inverse)
                if c == 0 and level < 3:
                    store(diag[level], (x,), y0, n, total)

        rows(HX[level] - radius, N[level] + 2 * radius, body, group)

    def normalise(level, radius, rhs=None):
        y0, n = lines(level, radius)
        rhs = b[level] if rhs is None else rhs

        def body(x, px):
            for c in (0, 1):
                store(norm[level], (c, x), y0, n, load(rhs, (c, x), y0, n) * load(coef[level], (6, c, x), y0, n))

        rows(HX[level] - radius, N[level] + 2 * radius, body, 24)

    def solved(level, c, x0, count, y0, n, other, lead=()):
        mids = [load(other, lead + (x0 + j - 1,), y0, n) for j in range(count + 2)]
        out = []
        for j in range(count):
            x = x0 + j
            kind = (c + j + y0) % 2
            factor = lambda k: load(coef[level], (k, c, x), y0, n)
            value = load(norm[level], (c, x), y0, n) + mids[j + 2] * factor(0)
            value2 = mids[j] * factor(1) + load(other, lead + (x,), y0 + 1, n) * factor(2)
            value3 = load(other, lead + (x,), y0 - 1, n) * factor(3) + mids[j + 1] * factor(4)
            out.append((kind, mids[j + 1], factor(5), (value + value2) + value3))
        return out

    def finish(out, px):
        return [total + beside(same, (kind + px) % 2) * factor for kind, same, factor, total in out]

    def chunks(x0, count, body, group):
        steps = count // group
        if steps > 1:

            def step(i, carry):
                body(x0 + i * group, x0 % 2, group)
                return carry

            lax.fori_loop(0, steps, step, 0)
            left = count - steps * group
        else:
            left = count
        if left:
            body(x0 + count - left, (x0 + count - left) % 2, left)

    def half_sweep(level, c, radius, other=None, lead=(), group=GROUP):
        y0, n = lines(level, radius)
        mine = (red_p, black_p)[c][level]
        other = (black_p, red_p)[c][level] if other is None else other

        def body(x, px, count):
            values = finish(solved(level, c, x, count, y0, n, other, lead), px)
            for j, value in enumerate(values):
                store(mine, (x + j,), y0, n, value)

        chunks(HX[level] - radius, N[level] + 2 * radius, body, group)

    def put_coarse(ref, level, i, even, odd):
        n = N[level]

        def put(parity):
            swapped = odd_rows(n, parity)
            here = (HX[level] + i, pl.ds(HY[level], n))
            ref[(0,) + here] = jnp.where(swapped, odd, even)
            ref[(1,) + here] = jnp.where(swapped, even, odd)

        return put

    def coarsen_beta(level):
        n = N[level + 1]

        def body(i, pi):
            def child(c, a, k):
                return beta[level][c, HX[level] + 2 * i + a, pl.ds(HY[level] + k, n, stride=2), :]

            even = 0.25 * ((child(0, 0, 0) + child(0, 1, 1)) + (child(1, 0, 1) + child(1, 1, 0)))
            odd = 0.25 * ((child(1, 0, 0) + child(1, 1, 1)) + (child(0, 0, 1) + child(0, 1, 0)))
            put_coarse(beta[level + 1], level + 1, i, even, odd)(pi)

        rows(0, n, body)

    def residual(level):
        n, nc = N[level], N[level + 1]
        y0, padded = lines(level, 0)

        def body(x, px, count):
            values = finish(solved(level, 0, x, count, y0, padded, black_p[level]), px)
            for j, value in enumerate(values):
                left = (value - load(red_p[level], (x + j,), y0, padded)) * load(diag[level], (x + j,), y0, padded)
                store(res, (x + j - HX[level],), 0, padded, left)
                field[level][x + j, pl.ds(y0, n)] = black_p[level][x + j, pl.ds(y0, n)]

        chunks(HX[level], n, body, GROUP)

        def restrict(i, pi):
            def child(a, k):
                return res[2 * i + a, pl.ds(k, nc, stride=2), :]

            put_coarse(b[level + 1], level + 1, i, 0.25 * (child(0, 0) + child(1, 1)), 0.25 * (child(0, 1) + child(1, 0)))(pi)

        rows(0, nc, restrict, 8)

    def prolong(level, x0, nx, y0, n, red):
        half = n // 2
        i0 = HX[level + 1] + (x0 - HX[level]) // 2
        j0 = HY[level + 1] + (y0 - HY[level]) // 2

        def body(i, pi):
            first, second = red[i, pl.ds(j0, half), :], black_p[level + 1][i, pl.ds(j0, half), :]
            swapped = odd_rows(half, j0 + pi)
            even, odd = jnp.where(swapped, second, first), jnp.where(swapped, first, second)
            for a in (0, 1):
                x = x0 + 2 * (i - i0) + a
                for k in (0, 1):
                    here = (x, pl.ds(y0 + k, half, stride=2), slice(None))
                    black_p[level][here] = field[level][here] + (odd if a == k else even)

        rows(i0, nx // 2, body, 12)

    def descend(level):
        half_sweep(level, 1, 3, norm[level], (0,))
        half_sweep(level, 0, 2)
        half_sweep(level, 1, 1)
        residual(level)

    barrier = pltpu.get_barrier_semaphore()
    for a, c in PARTNERS:
        pl.semaphore_signal(barrier, inc=1, device_id=device(a, c), device_id_type=MESH)
    fetch_inv = pltpu.make_async_copy(inv_hbm, inv_ref, load_sem.at[0])
    fetch_src = pltpu.make_async_copy(src_hbm, src_ref, load_sem.at[1])
    fetch_inv.start()
    fetch_src.start()

    wide = lax.broadcasted_iota(jnp.int32, (16, LANES), 1)

    def take(ref, to):
        def body(x, px):
            odd = odd_rows(16, px).astype(jnp.int32)
            low = wide < LANES // 2
            lower, upper = ref[x, :, pl.ds(0, LANES)], ref[x, :, pl.ds(LANES, LANES)]
            for c in (0, 1):
                slot = lax.rem(2 * wide + (odd if c == 0 else 1 - odd), LANES)
                value = jnp.where(low, jnp.take_along_axis(lower, slot, axis=1), jnp.take_along_axis(upper, slot, axis=1))
                to[c, HX[0] + x, pl.ds(HY[0], 16)] = value

        rows(0, 16, body, 16)

    fetch_inv.wait()
    take(inv_ref, beta[0])
    fetch_src.wait()
    take(src_ref, b[0])
    pl.semaphore_wait(barrier, len(PARTNERS))
    send("e0k")
    send("e0")
    send("b0")
    send("b0k")
    for level in (0, 1, 2):
        coarsen_beta(level)
    send("e1")
    send("e2x")
    receive("e0k", "e0")
    set_up(0, 4, 8)
    receive("b0", "b0k")
    normalise(0, 4)
    descend(0)

    send("b1")
    receive("e2x")
    send("e2y")
    send("e3x")
    send("f0x")
    receive("e1")
    set_up(1, 6, 4)
    receive("b1")
    normalise(1, 4)
    descend(1)

    send("b2")
    receive("e3x", "f0x")
    send("e3y")
    send("f1x")
    normalise(1, 6)
    receive("e2y")
    set_up(2, 7, 6)
    receive("b2")
    normalise(2, 4)
    descend(2)

    send("b3")
    send("f2x")
    send("b2far")
    receive("f1x")
    send("f1y")
    send("f0y")
    receive("e3y")
    set_up(3, 6, 14)
    receive("b3")
    normalise(3, 6)
    half_sweep(3, 1, 5, norm[3], (0,))
    for step in range(2, 7):
        half_sweep(3, step % 2, 6 - step)
    for x in range(HX[3], HX[3] + N[3]):
        field[3][x, pl.ds(HY[3], N[3])] = red_p[3][x, pl.ds(HY[3], N[3])]
    send("f3")
    receive("f2x")
    send("f2y")

    def keep_rhs(x, px):
        for c in (0, 1):
            b2w[c, x, pl.ds(6, 12)] = b[2][c, x, pl.ds(6, 12)]

    rows(4, 12, keep_rhs, 6)
    for name in NAMES:
        if name not in ("f2y", "f3"):
            await_bytes(send_sem, name)
    receive("b2far")
    normalise(2, 7, b2w)
    receive("f3")
    half_sweep(3, 1, 5, field[3])

    receive("f2y")
    prolong(2, 0, 20, 2, 24, field[3])
    for step in range(4):
        half_sweep(2, step % 2, 7 - step)
    receive("f1y")
    prolong(1, 0, 24, 2, 24, red_p[2])
    for step in range(4):
        half_sweep(1, step % 2, 6 - step)
    receive("f0y")
    prolong(0, 2, 24, 2, 24, red_p[1])
    for step in range(4):
        half_sweep(0, step % 2, 3 - step)

    def give(x, px):
        red, black = red_p[0][HX[0] + x, pl.ds(HY[0], 16)], black_p[0][HX[0] + x, pl.ds(HY[0], 16)]
        is_red = (wide + odd_rows(16, px).astype(jnp.int32)) % 2 == 0
        for part in (0, 1):
            slot = wide // 2 + part * (LANES // 2)
            out_ref[x, :, pl.ds(part * LANES, LANES)] = jnp.where(
                is_red, jnp.take_along_axis(red, slot, axis=1), jnp.take_along_axis(black, slot, axis=1))

    rows(0, 16, give, 16)
    for name in ("f2y", "f3"):
        await_bytes(send_sem, name)


def solution(mesh):
    gx_size, gy_size = mesh.shape["gx"], mesh.shape["gy"]

    def both(level):
        return pltpu.VMEM((2, XE[level], YE[level], LANES), jnp.float32)

    def single(level):
        return pltpu.VMEM((XE[level], YE[level], LANES), jnp.float32)

    levels = range(4)
    block = pltpu.VMEM((16, 16, 2 * LANES), jnp.float32)
    scratch = [both(level) for _ in range(3) for level in levels]
    scratch += [single(level) for _ in range(2) for level in levels]
    scratch += [pltpu.VMEM((7, 2, XE[level], YE[level], LANES), jnp.float32) for level in levels]
    scratch += [single(level) for level in range(3)] + [single(level) for level in levels]
    scratch += [both(2), pltpu.VMEM((16, 16, LANES), jnp.float32), block, block]
    scratch += [pltpu.VMEM((MOST, LANES), jnp.float32), pltpu.SemaphoreType.DMA((2,))]
    scratch += [pltpu.SemaphoreType.DMA((len(NAMES),))] * 2

    def on_device(source, inv_density):
        hbm = pl.BlockSpec(memory_space=pltpu.HBM)

        def body(*refs):
            kernel(gx_size, gy_size, *refs)

        return pl.pallas_call(
            body,
            out_shape=pltpu.VMEM(source.shape, jnp.float32),
            in_specs=[hbm, hbm],
            out_specs=pl.BlockSpec(memory_space=pltpu.VMEM),
            scratch_shapes=scratch,
            name="v_cycle",
            compiler_params=pltpu.CompilerParams(
                collective_id=0, has_side_effects=True, vmem_limit_bytes=60 << 20
            ),
        )(source, inv_density)

    placed = P("gx", "gy", None)
    return jax.shard_map(
        on_device, mesh=mesh, in_specs=(placed, placed), out_specs=placed, check_vma=False
    )
```

```python
import jax
import jax.numpy as jnp
from jax import lax
from jax.experimental import pallas as pl
from jax.experimental.pallas import tpu as pltpu
from jax.sharding import PartitionSpec as P


MESH = pl.DeviceIdType.MESH
N = (16, 8, 4, 2)
HX = (6, 8, 8, 8)
HY = (6, 10, 10, 8)
XE = (28, 24, 20, 18)
YE = (32, 32, 32, 24)
WH = (0.5, 0.125, 0.03125, 0.0078125)
WV = 0.125
LANES = 128
GROUP = 24


def spread(n, radius, keep=None):
    out = []
    reach = -(-radius // n)
    for a in range(-reach, reach + 1):
        for b in range(-reach, reach + 1):
            gap_x = (abs(a) - 1) * n + 1 if a else 0
            gap_y = (abs(b) - 1) * n + 1 if b else 0
            if (a, b) == (0, 0) or gap_x + gap_y > radius:
                continue
            if keep is not None and not keep(a, b):
                continue
            rx, ry = radius - gap_y, radius - gap_x
            x0, x1 = max(-a * n, -rx), min(-a * n + n, n + rx)
            y0, y1 = max(-b * n, -ry), min(-b * n + n, n + ry)
            out.append((a, b, x0, x1 - x0, y0, y1 - y0))
    if n == 2:
        return sorted(out, key=lambda m: -(2 * abs(m[0]) + abs(m[1])))
    return sorted(out, key=lambda m: (m[1] != 0, m[0] == 0))


def along_x(n, radius):
    return [m for m in spread(n, radius) if m[1] == 0]


def along_y(n, radius):
    out = []
    for _, c, _, _, y0, ny in [m for m in spread(n, radius) if m[0] == 0]:
        width = radius - ((abs(c) - 1) * n + 1)
        out.append((0, c, -width, n + 2 * width, y0, ny))
    return out


def near(a, b):
    return max(abs(a), abs(b)) == 1


BOTH, ONE, RED, BLACK = (slice(None),), (), (0,), (1,)
GROUPS = {
    "b0": (0, RED, spread(16, 4)),
    "b0k": (0, BLACK, spread(16, 3)),
    "e0": (0, RED, spread(16, 4)),
    "e0k": (0, BLACK, spread(16, 5)),
    "e1x": (1, BOTH, along_x(8, 7)),
    "e1y": (1, BOTH, along_y(8, 7)),
    "e2x": (2, BOTH, along_x(4, 8)),
    "e2y": (2, BOTH, along_y(4, 8)),
    "e3x": (3, BOTH, along_x(2, 7)),
    "e3y": (3, BOTH, along_y(2, 7)),
    "f0x": (0, ONE, along_x(16, 4)),
    "f0y": (0, ONE, along_y(16, 4)),
    "b1": (1, BOTH, spread(8, 4)),
    "b1x": (1, BOTH, along_x(8, 6)),
    "b1y": (1, BOTH, along_y(8, 6)),
    "f1x": (1, ONE, along_x(8, 7)),
    "f1y": (1, ONE, along_y(8, 7)),
    "b2": (2, BOTH, spread(4, 4)),
    "b2x": (2, BOTH, along_x(4, 7)),
    "b2y": (2, BOTH, along_y(4, 7)),
    "f2x": (2, ONE, along_x(4, 8)),
    "f2y": (2, ONE, along_y(4, 8)),
    "b3": (3, BOTH, spread(2, 6)),
    "f3": (3, ONE, spread(2, 6)),
}
NAMES = tuple(GROUPS)
COUNT = {k: (2 if c == BOTH else 1) * sum(m[3] * m[5] for m in msgs) for k, (_, c, msgs) in GROUPS.items()}
MOST = -(-max(COUNT.values()) // 8) * 8
PARTNERS = [m[:2] for m in spread(1, 2, near)] + [(a, 0) for a in (-4, -3, -2, 2, 3, 4)] + [(0, -4), (0, 4)]


def rows(x0, nx, body, group=4):
    steps = nx // group
    if steps > 1:

        def step(i, carry):
            for j in range(group):
                body(x0 + i * group + j, (x0 + j) % 2)
            return carry

        lax.fori_loop(0, steps, step, 0)
        done = steps * group
    else:
        done = 0
    for j in range(done, nx):
        body(x0 + j, (x0 + j) % 2)


def odd_rows(n, offset):
    return (lax.broadcasted_iota(jnp.int32, (n, LANES), 0) + offset) % 2 == 1


def lines(level, radius):
    return HY[level] - radius, -(-(N[level] + 2 * radius) // 8) * 8


def kernel(gx_size, gy_size, src_hbm, inv_hbm, out_ref, *scratch):
    beta, b, norm, red_p, black_p, coef = (scratch[4 * k : 4 * k + 4] for k in range(6))
    diag, field = scratch[24:27], scratch[27:31]
    b1w, b2w, res, src_ref, inv_ref, dummy, load_sem, send_sem, recv_sem = scratch[31:]
    sent = {"b1x": b[1], "b1y": b1w, "b2x": b[2], "b2y": b2w, "b0k": b[0], "e0k": beta[0]}
    for level in range(4):
        for end in ("", "x", "y"):
            sent.update({"e%d%s" % (level, end): beta[level], "f%d%s" % (level, end): field[level]})
        sent["b%d" % level] = b[level]
    landed = dict(sent, b1x=b1w, b2x=b2w)

    ix, iy = lax.axis_index("gx"), lax.axis_index("gy")
    at_x = {a: lax.rem(ix + (a + gx_size), gx_size) for a in range(-4, 5)}
    at_y = {a: lax.rem(iy + (a + gy_size), gy_size) for a in range(-4, 5)}

    def device(a, c):
        return {"gx": at_x[a], "gy": at_y[c]}

    def send(name):
        level, colours, msgs = GROUPS[name]
        k, n = NAMES.index(name), N[level]
        for a, c, x0, nx, y0, ny in msgs:
            here = (pl.ds(HX[level] + x0 + a * n, nx), pl.ds(HY[level] + y0 + c * n, ny))
            there = (pl.ds(HX[level] + x0, nx), pl.ds(HY[level] + y0, ny))
            here, there = colours + here, colours + there
            pltpu.make_async_remote_copy(
                src_ref=sent[name].at[here], dst_ref=landed[name].at[there],
                send_sem=send_sem.at[k], recv_sem=recv_sem.at[k],
                device_id=device(a, c), device_id_type=MESH,
            ).start()

    def await_bytes(sem, name):
        block = dummy.at[pl.ds(0, COUNT[name])]
        pltpu.make_async_copy(block, block, sem.at[NAMES.index(name)]).wait()

    def receive(*names):
        for name in names:
            await_bytes(recv_sem, name)

    lane = lax.broadcasted_iota(jnp.int32, (8, LANES), 1)
    odd8 = odd_rows(8, 0)

    def weights(kind):
        down = jnp.logical_not(odd8) if kind == 0 else odd8
        has = jnp.where(down, jnp.where(lane > 0, 1.0, 0.0), jnp.where(lane < LANES - 1, 1.0, 0.0))
        return jnp.where(down, 1.0, 0.0)[None], has[None]

    weight = (weights(0), weights(1))

    def load(ref, lead, y0, n):
        return ref[lead + (pl.ds(y0, n),)].reshape(n // 8, 8, LANES)

    def store(ref, lead, y0, n, value):
        ref[lead + (pl.ds(y0, n),)] = value.reshape(n, LANES)

    def beside(same, kind):
        flat = same.reshape(-1, LANES)
        lower = pltpu.roll(flat, 1, 1).reshape(same.shape)
        upper = pltpu.roll(flat, LANES - 1, 1).reshape(same.shape)
        return jnp.where(weight[kind][0] > 0.0, lower, upper)

    def set_up(level, radius, group):
        wh = WH[level]
        y0, n = lines(level, radius)

        def body(x, px):
            for c in (0, 1):
                kind = (c + px + y0) % 2
                at = lambda dx, dy: load(beta[level], (1 - c, x + dx), y0 + dy, n)
                centre, same = load(beta[level], (c, x), y0, n), at(0, 0)
                has = weight[kind][1]
                other = beside(same, kind)
                other = other * has + centre * (1.0 - has)
                sides = (at(1, 0), at(-1, 0), at(0, 1), at(0, -1))
                total = centre * (4 * wh + 2 * WV) + wh * ((sides[0] + sides[1]) + (sides[2] + sides[3])) + WV * (same + other)
                inverse = 1.0 / total
                across, upright = wh * inverse, WV * inverse
                for k, side in enumerate(sides):
                    store(coef[level], (k, c, x), y0, n, (centre + side) * across)
                store(coef[level], (4, c, x), y0, n, (centre + same) * upright)
                store(coef[level], (5, c, x), y0, n, (centre + other) * (upright * has))
                store(coef[level], (6, c, x), y0, n, inverse)
                if c == 0 and level < 3:
                    store(diag[level], (x,), y0, n, total)

        rows(HX[level] - radius, N[level] + 2 * radius, body, group)

    def normalise(level, radius, rhs=None):
        y0, n = lines(level, radius)
        rhs = b[level] if rhs is None else rhs

        def body(x, px):
            for c in (0, 1):
                store(norm[level], (c, x), y0, n, load(rhs, (c, x), y0, n) * load(coef[level], (6, c, x), y0, n))

        rows(HX[level] - radius, N[level] + 2 * radius, body, 24)

    def solved(level, c, x0, count, y0, n, other, lead=()):
        mids = [load(other, lead + (x0 + j - 1,), y0, n) for j in range(count + 2)]
        out = []
        for j in range(count):
            x = x0 + j
            kind = (c + j + y0) % 2
            factor = lambda k: load(coef[level], (k, c, x), y0, n)
            value = load(norm[level], (c, x), y0, n) + mids[j + 2] * factor(0)
            value2 = mids[j] * factor(1) + load(other, lead + (x,), y0 + 1, n) * factor(2)
            value3 = load(other, lead + (x,), y0 - 1, n) * factor(3) + mids[j + 1] * factor(4)
            out.append((kind, mids[j + 1], factor(5), (value + value2) + value3))
        return out

    def finish(out, px):
        return [total + beside(same, (kind + px) % 2) * factor for kind, same, factor, total in out]

    def chunks(x0, count, body, group):
        steps = count // group
        if steps > 1:

            def step(i, carry):
                body(x0 + i * group, x0 % 2, group)
                return carry

            lax.fori_loop(0, steps, step, 0)
            left = count - steps * group
        else:
            left = count
        if left:
            body(x0 + count - left, (x0 + count - left) % 2, left)

    def half_sweep(level, c, radius, other=None, lead=(), group=GROUP):
        y0, n = lines(level, radius)
        mine = (red_p, black_p)[c][level]
        other = (black_p, red_p)[c][level] if other is None else other

        def body(x, px, count):
            values = finish(solved(level, c, x, count, y0, n, other, lead), px)
            for j, value in enumerate(values):
                store(mine, (x + j,), y0, n, value)

        chunks(HX[level] - radius, N[level] + 2 * radius, body, group)

    def put_coarse(ref, level, i, even, odd):
        n = N[level]

        def put(parity):
            swapped = odd_rows(n, parity)
            here = (HX[level] + i, pl.ds(HY[level], n))
            ref[(0,) + here] = jnp.where(swapped, odd, even)
            ref[(1,) + here] = jnp.where(swapped, even, odd)

        return put

    def coarsen_beta(level):
        n = N[level + 1]

        def body(i, pi):
            def child(c, a, k):
                return beta[level][c, HX[level] + 2 * i + a, pl.ds(HY[level] + k, n, stride=2), :]

            even = 0.25 * ((child(0, 0, 0) + child(0, 1, 1)) + (child(1, 0, 1) + child(1, 1, 0)))
            odd = 0.25 * ((child(1, 0, 0) + child(1, 1, 1)) + (child(0, 0, 1) + child(0, 1, 0)))
            put_coarse(beta[level + 1], level + 1, i, even, odd)(pi)

        rows(0, n, body)

    def residual(level):
        n, nc = N[level], N[level + 1]
        y0, padded = lines(level, 0)

        def body(x, px, count):
            values = finish(solved(level, 0, x, count, y0, padded, black_p[level]), px)
            for j, value in enumerate(values):
                left = (value - load(red_p[level], (x + j,), y0, padded)) * load(diag[level], (x + j,), y0, padded)
                store(res, (x + j - HX[level],), 0, padded, left)
                field[level][x + j, pl.ds(y0, n)] = black_p[level][x + j, pl.ds(y0, n)]

        chunks(HX[level], n, body, GROUP)

        def restrict(i, pi):
            def child(a, k):
                return res[2 * i + a, pl.ds(k, nc, stride=2), :]

            put_coarse(b[level + 1], level + 1, i, 0.25 * (child(0, 0) + child(1, 1)), 0.25 * (child(0, 1) + child(1, 0)))(pi)

        rows(0, nc, restrict, 8)

    def prolong(level, x0, nx, y0, n, red):
        half = n // 2
        i0 = HX[level + 1] + (x0 - HX[level]) // 2
        j0 = HY[level + 1] + (y0 - HY[level]) // 2

        def body(i, pi):
            first, second = red[i, pl.ds(j0, half), :], black_p[level + 1][i, pl.ds(j0, half), :]
            swapped = odd_rows(half, j0 + pi)
            even, odd = jnp.where(swapped, second, first), jnp.where(swapped, first, second)
            for a in (0, 1):
                x = x0 + 2 * (i - i0) + a
                for k in (0, 1):
                    here = (x, pl.ds(y0 + k, half, stride=2), slice(None))
                    black_p[level][here] = field[level][here] + (odd if a == k else even)

        rows(i0, nx // 2, body, 12)

    def keep_own(level, to):
        def body(x, px):
            for c in (0, 1):
                here = (c, HX[level] + x, pl.ds(HY[level], N[level]))
                to[here] = b[level][here]

        rows(0, N[level], body, 8)

    def descend(level):
        half_sweep(level, 1, 3, norm[level], (0,))
        half_sweep(level, 0, 2)
        half_sweep(level, 1, 1)
        residual(level)

    barrier = pltpu.get_barrier_semaphore()
    fetch_inv = pltpu.make_async_copy(inv_hbm, inv_ref, load_sem.at[0])
    fetch_src = pltpu.make_async_copy(src_hbm, src_ref, load_sem.at[1])
    fetch_inv.start()
    fetch_src.start()
    for a, c in PARTNERS:
        pl.semaphore_signal(barrier, inc=1, device_id=device(a, c), device_id_type=MESH)

    wide = lax.broadcasted_iota(jnp.int32, (16, LANES), 1)

    def take(ref, to):
        def body(x, px):
            odd = odd_rows(16, px).astype(jnp.int32)
            low = wide < LANES // 2
            lower, upper = ref[x, :, pl.ds(0, LANES)], ref[x, :, pl.ds(LANES, LANES)]
            for c in (0, 1):
                slot = lax.rem(2 * wide + (odd if c == 0 else 1 - odd), LANES)
                value = jnp.where(low, jnp.take_along_axis(lower, slot, axis=1), jnp.take_along_axis(upper, slot, axis=1))
                to[c, HX[0] + x, pl.ds(HY[0], 16)] = value

        rows(0, 16, body, 16)

    fetch_inv.wait()
    take(inv_ref, beta[0])
    fetch_src.wait()
    take(src_ref, b[0])
    pl.semaphore_wait(barrier, len(PARTNERS))
    send("e0k")
    send("e0")
    send("b0")
    send("b0k")
    for level in (0, 1, 2):
        coarsen_beta(level)
    send("e1x")
    send("e2x")
    receive("e0k", "e0")
    set_up(0, 4, 8)
    receive("b0", "b0k")
    normalise(0, 4)
    descend(0)

    send("b1")
    receive("e1x", "e2x")
    send("e1y")
    send("e2y")
    send("b1x")
    send("e3x")
    send("f0x")
    keep_own(1, b1w)
    receive("e1y")
    set_up(1, 6, 4)
    receive("b1")
    normalise(1, 4)
    descend(1)

    send("b2")
    receive("e3x", "f0x", "b1x")
    send("e3y")
    send("f1x")
    send("b1y")
    keep_own(2, b2w)
    receive("e2y")
    set_up(2, 7, 6)
    receive("b2")
    normalise(2, 4)
    descend(2)

    send("b3")
    send("f2x")
    send("b2x")
    receive("f1x")
    send("f1y")
    send("f0y")
    receive("e3y")
    set_up(3, 6, 14)
    receive("b3")
    normalise(3, 6)
    half_sweep(3, 1, 5, norm[3], (0,))
    for step in range(2, 7):
        half_sweep(3, step % 2, 6 - step)
    for x in range(HX[3], HX[3] + N[3]):
        field[3][x, pl.ds(HY[3], N[3])] = red_p[3][x, pl.ds(HY[3], N[3])]
    send("f3")
    receive("f2x", "b2x")
    send("f2y")
    send("b2y")

    for name in NAMES:
        if name not in ("b2y", "f2y", "f3"):
            await_bytes(send_sem, name)
    receive("b1y")
    normalise(1, 6, b1w)
    receive("b2y")
    normalise(2, 7, b2w)
    receive("f3")
    half_sweep(3, 1, 5, field[3])

    receive("f2y")
    prolong(2, 0, 20, 2, 24, field[3])
    for step in range(4):
        half_sweep(2, step % 2, 7 - step)
    receive("f1y")
    prolong(1, 0, 24, 2, 24, red_p[2])
    for step in range(4):
        half_sweep(1, step % 2, 6 - step)
    receive("f0y")
    prolong(0, 2, 24, 2, 24, red_p[1])
    for step in range(4):
        half_sweep(0, step % 2, 3 - step)

    def give(x, px):
        red, black = red_p[0][HX[0] + x, pl.ds(HY[0], 16)], black_p[0][HX[0] + x, pl.ds(HY[0], 16)]
        is_red = (wide + odd_rows(16, px).astype(jnp.int32)) % 2 == 0
        for part in (0, 1):
            slot = wide // 2 + part * (LANES // 2)
            out_ref[x, :, pl.ds(part * LANES, LANES)] = jnp.where(
                is_red, jnp.take_along_axis(red, slot, axis=1), jnp.take_along_axis(black, slot, axis=1))

    rows(0, 16, give, 16)
    for name in ("b2y", "f2y", "f3"):
        await_bytes(send_sem, name)


def solution(mesh):
    gx_size, gy_size = mesh.shape["gx"], mesh.shape["gy"]

    def both(level):
        return pltpu.VMEM((2, XE[level], YE[level], LANES), jnp.float32)

    def single(level):
        return pltpu.VMEM((XE[level], YE[level], LANES), jnp.float32)

    levels = range(4)
    block = pltpu.VMEM((16, 16, 2 * LANES), jnp.float32)
    scratch = [both(level) for _ in range(3) for level in levels]
    scratch += [single(level) for _ in range(2) for level in levels]
    scratch += [pltpu.VMEM((7, 2, XE[level], YE[level], LANES), jnp.float32) for level in levels]
    scratch += [single(level) for level in range(3)] + [single(level) for level in levels]
    scratch += [both(1), both(2), pltpu.VMEM((16, 16, LANES), jnp.float32), block, block]
    scratch += [pltpu.VMEM((MOST, LANES), jnp.float32), pltpu.SemaphoreType.DMA((2,))]
    scratch += [pltpu.SemaphoreType.DMA((len(NAMES),))] * 2

    def on_device(source, inv_density):
        hbm = pl.BlockSpec(memory_space=pltpu.HBM)

        def body(*refs):
            kernel(gx_size, gy_size, *refs)

        return pl.pallas_call(
            body,
            out_shape=pltpu.VMEM(source.shape, jnp.float32),
            in_specs=[hbm, hbm],
            out_specs=pl.BlockSpec(memory_space=pltpu.VMEM),
            scratch_shapes=scratch,
            name="v_cycle",
            compiler_params=pltpu.CompilerParams(
                collective_id=0, has_side_effects=True, vmem_limit_bytes=60 << 20
            ),
        )(source, inv_density)

    placed = P("gx", "gy", None)
    return jax.shard_map(
        on_device, mesh=mesh, in_specs=(placed, placed), out_specs=placed, check_vma=False
    )
```

```python
import jax
import jax.numpy as jnp
from jax import lax
from jax.experimental import pallas as pl
from jax.experimental.pallas import tpu as pltpu
from jax.sharding import PartitionSpec as P


MESH = pl.DeviceIdType.MESH
N = (16, 8, 4, 2)
HX = (6, 8, 8, 8)
HY = (6, 10, 10, 8)
XE = (28, 24, 20, 18)
YE = (32, 32, 32, 24)
WH = (0.5, 0.125, 0.03125, 0.0078125)
WV = 0.125
LANES = 128
GROUP = 24


def spread(n, radius, keep=None):
    out = []
    reach = -(-radius // n)
    for a in range(-reach, reach + 1):
        for b in range(-reach, reach + 1):
            gap_x = (abs(a) - 1) * n + 1 if a else 0
            gap_y = (abs(b) - 1) * n + 1 if b else 0
            if (a, b) == (0, 0) or gap_x + gap_y > radius:
                continue
            if keep is not None and not keep(a, b):
                continue
            rx, ry = radius - gap_y, radius - gap_x
            x0, x1 = max(-a * n, -rx), min(-a * n + n, n + rx)
            y0, y1 = max(-b * n, -ry), min(-b * n + n, n + ry)
            out.append((a, b, x0, x1 - x0, y0, y1 - y0))
    if n == 2:
        return sorted(out, key=lambda m: -(2 * abs(m[0]) + abs(m[1])))
    return sorted(out, key=lambda m: (m[1] != 0, m[0] == 0))


def along_x(n, radius):
    return [m for m in spread(n, radius) if m[1] == 0]


def along_y(n, radius):
    out = []
    for _, c, _, _, y0, ny in [m for m in spread(n, radius) if m[0] == 0]:
        width = radius - ((abs(c) - 1) * n + 1)
        out.append((0, c, -width, n + 2 * width, y0, ny))
    return out


def near(a, b):
    return max(abs(a), abs(b)) == 1


BOTH, ONE, RED, BLACK = (slice(None),), (), (0,), (1,)
GROUPS = {
    "b0": (0, RED, spread(16, 4)),
    "b0k": (0, BLACK, spread(16, 3)),
    "e0": (0, RED, spread(16, 4)),
    "e0k": (0, BLACK, spread(16, 5)),
    "e1x": (1, BOTH, along_x(8, 7)),
    "e1y": (1, BOTH, along_y(8, 7)),
    "e2x": (2, BOTH, along_x(4, 8)),
    "e2y": (2, BOTH, along_y(4, 8)),
    "e3x": (3, BOTH, along_x(2, 7)),
    "e3y": (3, BOTH, along_y(2, 7)),
    "f0x": (0, ONE, along_x(16, 4)),
    "f0y": (0, ONE, along_y(16, 4)),
    "b1": (1, BOTH, spread(8, 4)),
    "b1x": (1, BOTH, along_x(8, 6)),
    "b1y": (1, BOTH, along_y(8, 6)),
    "f1x": (1, ONE, along_x(8, 7)),
    "f1y": (1, ONE, along_y(8, 7)),
    "b2": (2, BOTH, spread(4, 4)),
    "b2x": (2, BOTH, along_x(4, 7)),
    "b2y": (2, BOTH, along_y(4, 7)),
    "f2x": (2, ONE, along_x(4, 8)),
    "f2y": (2, ONE, along_y(4, 8)),
    "b3": (3, BOTH, spread(2, 6)),
    "f3": (3, ONE, spread(2, 6)),
}
NAMES = tuple(GROUPS)
COUNT = {k: (2 if c == BOTH else 1) * sum(m[3] * m[5] for m in msgs) for k, (_, c, msgs) in GROUPS.items()}
MOST = -(-max(COUNT.values()) // 8) * 8
PARTNERS = [m[:2] for m in spread(1, 2, near)] + [(a, 0) for a in (-4, -3, -2, 2, 3, 4)] + [(0, -4), (0, 4)]


def rows(x0, nx, body, group=4):
    steps = nx // group
    if steps > 1:

        def step(i, carry):
            for j in range(group):
                body(x0 + i * group + j, (x0 + j) % 2)
            return carry

        lax.fori_loop(0, steps, step, 0)
        done = steps * group
    else:
        done = 0
    for j in range(done, nx):
        body(x0 + j, (x0 + j) % 2)


def odd_rows(n, offset):
    return (lax.broadcasted_iota(jnp.int32, (n, LANES), 0) + offset) % 2 == 1


def lines(level, radius):
    return HY[level] - radius, -(-(N[level] + 2 * radius) // 8) * 8


def kernel(gx_size, gy_size, src_hbm, inv_hbm, out_ref, *scratch):
    beta, b, norm, red_p, black_p, coef = (scratch[4 * k : 4 * k + 4] for k in range(6))
    diag, field = scratch[24:27], scratch[27:31]
    b1w, b2w, res, src_ref, inv_ref, dummy, load_sem, send_sem, recv_sem = scratch[31:]
    sent = {"b1x": b[1], "b1y": b1w, "b2x": b[2], "b2y": b2w, "b0k": b[0], "e0k": beta[0]}
    for level in range(4):
        for end in ("", "x", "y"):
            sent.update({"e%d%s" % (level, end): beta[level], "f%d%s" % (level, end): field[level]})
        sent["b%d" % level] = b[level]
    landed = dict(sent, b1x=b1w, b2x=b2w)

    ix, iy = lax.axis_index("gx"), lax.axis_index("gy")
    at_x = {a: lax.rem(ix + (a + gx_size), gx_size) for a in range(-4, 5)}
    at_y = {a: lax.rem(iy + (a + gy_size), gy_size) for a in range(-4, 5)}

    def device(a, c):
        return {"gx": at_x[a], "gy": at_y[c]}

    def send(name):
        level, colours, msgs = GROUPS[name]
        k, n = NAMES.index(name), N[level]
        for a, c, x0, nx, y0, ny in msgs:
            here = (pl.ds(HX[level] + x0 + a * n, nx), pl.ds(HY[level] + y0 + c * n, ny))
            there = (pl.ds(HX[level] + x0, nx), pl.ds(HY[level] + y0, ny))
            here, there = colours + here, colours + there
            pltpu.make_async_remote_copy(
                src_ref=sent[name].at[here], dst_ref=landed[name].at[there],
                send_sem=send_sem.at[k], recv_sem=recv_sem.at[k],
                device_id=device(a, c), device_id_type=MESH,
            ).start()

    def await_bytes(sem, name):
        block = dummy.at[pl.ds(0, COUNT[name])]
        pltpu.make_async_copy(block, block, sem.at[NAMES.index(name)]).wait()

    def receive(*names):
        for name in names:
            await_bytes(recv_sem, name)

    lane = lax.broadcasted_iota(jnp.int32, (8, LANES), 1)
    odd8 = odd_rows(8, 0)

    def weights(kind):
        down = jnp.logical_not(odd8) if kind == 0 else odd8
        has = jnp.where(down, jnp.where(lane > 0, 1.0, 0.0), jnp.where(lane < LANES - 1, 1.0, 0.0))
        return jnp.where(down, 1.0, 0.0)[None], has[None]

    weight = (weights(0), weights(1))

    def load(ref, lead, y0, n):
        return ref[lead + (pl.ds(y0, n),)].reshape(n // 8, 8, LANES)

    def store(ref, lead, y0, n, value):
        ref[lead + (pl.ds(y0, n),)] = value.reshape(n, LANES)

    def beside(same, kind):
        flat = same.reshape(-1, LANES)
        lower = pltpu.roll(flat, 1, 1).reshape(same.shape)
        upper = pltpu.roll(flat, LANES - 1, 1).reshape(same.shape)
        return jnp.where(weight[kind][0] > 0.0, lower, upper)

    def set_up(level, radius, group):
        wh = WH[level]
        y0, n = lines(level, radius)

        def body(x, px):
            for c in (0, 1):
                kind = (c + px + y0) % 2
                at = lambda dx, dy: load(beta[level], (1 - c, x + dx), y0 + dy, n)
                centre, same = load(beta[level], (c, x), y0, n), at(0, 0)
                has = weight[kind][1]
                other = beside(same, kind)
                other = other * has + centre * (1.0 - has)
                sides = (at(1, 0), at(-1, 0), at(0, 1), at(0, -1))
                total = centre * (4 * wh + 2 * WV) + wh * ((sides[0] + sides[1]) + (sides[2] + sides[3])) + WV * (same + other)
                inverse = 1.0 / total
                across, upright = wh * inverse, WV * inverse
                for k, side in enumerate(sides):
                    store(coef[level], (k, c, x), y0, n, (centre + side) * across)
                store(coef[level], (4, c, x), y0, n, (centre + same) * upright)
                store(coef[level], (5, c, x), y0, n, (centre + other) * (upright * has))
                store(coef[level], (6, c, x), y0, n, inverse)
                if c == 0 and level < 3:
                    store(diag[level], (x,), y0, n, total)

        rows(HX[level] - radius, N[level] + 2 * radius, body, group)

    def normalise(level, radius, rhs=None):
        y0, n = lines(level, radius)
        rhs = b[level] if rhs is None else rhs

        def body(x, px):
            for c in (0, 1):
                store(norm[level], (c, x), y0, n, load(rhs, (c, x), y0, n) * load(coef[level], (6, c, x), y0, n))

        rows(HX[level] - radius, N[level] + 2 * radius, body, 24)

    def solved(level, c, x0, count, y0, n, other, lead=()):
        mids = [load(other, lead + (x0 + j - 1,), y0, n) for j in range(count + 2)]
        out = []
        for j in range(count):
            x = x0 + j
            kind = (c + j + y0) % 2
            factor = lambda k: load(coef[level], (k, c, x), y0, n)
            value = load(norm[level], (c, x), y0, n) + mids[j + 2] * factor(0)
            value2 = mids[j] * factor(1) + load(other, lead + (x,), y0 + 1, n) * factor(2)
            value3 = load(other, lead + (x,), y0 - 1, n) * factor(3) + mids[j + 1] * factor(4)
            out.append((kind, mids[j + 1], factor(5), (value + value2) + value3))
        return out

    def finish(out, px):
        return [total + beside(same, (kind + px) % 2) * factor for kind, same, factor, total in out]

    def chunks(x0, count, body, group):
        steps = count // group
        if steps > 1:

            def step(i, carry):
                body(x0 + i * group, x0 % 2, group)
                return carry

            lax.fori_loop(0, steps, step, 0)
            left = count - steps * group
        else:
            left = count
        if left:
            body(x0 + count - left, (x0 + count - left) % 2, left)

    def half_sweep(level, c, radius, other=None, lead=(), group=GROUP):
        y0, n = lines(level, radius)
        mine = (red_p, black_p)[c][level]
        other = (black_p, red_p)[c][level] if other is None else other

        def body(x, px, count):
            values = finish(solved(level, c, x, count, y0, n, other, lead), px)
            for j, value in enumerate(values):
                store(mine, (x + j,), y0, n, value)

        chunks(HX[level] - radius, N[level] + 2 * radius, body, group)

    def put_coarse(ref, level, i, even, odd):
        n = N[level]

        def put(parity):
            swapped = odd_rows(n, parity)
            here = (HX[level] + i, pl.ds(HY[level], n))
            ref[(0,) + here] = jnp.where(swapped, odd, even)
            ref[(1,) + here] = jnp.where(swapped, even, odd)

        return put

    def coarsen_beta(level):
        n = N[level + 1]

        def body(i, pi):
            def child(c, a, k):
                return beta[level][c, HX[level] + 2 * i + a, pl.ds(HY[level] + k, n, stride=2), :]

            even = 0.25 * ((child(0, 0, 0) + child(0, 1, 1)) + (child(1, 0, 1) + child(1, 1, 0)))
            odd = 0.25 * ((child(1, 0, 0) + child(1, 1, 1)) + (child(0, 0, 1) + child(0, 1, 0)))
            put_coarse(beta[level + 1], level + 1, i, even, odd)(pi)

        rows(0, n, body)

    def residual(level):
        n, nc = N[level], N[level + 1]
        y0, padded = lines(level, 0)

        def body(x, px, count):
            values = finish(solved(level, 0, x, count, y0, padded, black_p[level]), px)
            for j, value in enumerate(values):
                left = (value - load(red_p[level], (x + j,), y0, padded)) * load(diag[level], (x + j,), y0, padded)
                store(res, (x + j - HX[level],), 0, padded, left)
                field[level][x + j, pl.ds(y0, n)] = black_p[level][x + j, pl.ds(y0, n)]

        chunks(HX[level], n, body, GROUP)

        def restrict(i, pi):
            def child(a, k):
                return res[2 * i + a, pl.ds(k, nc, stride=2), :]

            put_coarse(b[level + 1], level + 1, i, 0.25 * (child(0, 0) + child(1, 1)), 0.25 * (child(0, 1) + child(1, 0)))(pi)

        rows(0, nc, restrict, 8)

    def prolong(level, x0, nx, y0, n, red):
        half = n // 2
        i0 = HX[level + 1] + (x0 - HX[level]) // 2
        j0 = HY[level + 1] + (y0 - HY[level]) // 2

        def body(i, pi):
            first, second = red[i, pl.ds(j0, half), :], black_p[level + 1][i, pl.ds(j0, half), :]
            swapped = odd_rows(half, j0 + pi)
            even, odd = jnp.where(swapped, second, first), jnp.where(swapped, first, second)
            for a in (0, 1):
                x = x0 + 2 * (i - i0) + a
                for k in (0, 1):
                    here = (x, pl.ds(y0 + k, half, stride=2), slice(None))
                    black_p[level][here] = field[level][here] + (odd if a == k else even)

        rows(i0, nx // 2, body, 12)

    def keep_own(level, to):
        def body(x, px):
            for c in (0, 1):
                here = (c, HX[level] + x, pl.ds(HY[level], N[level]))
                to[here] = b[level][here]

        rows(0, N[level], body, 8)

    def descend(level):
        half_sweep(level, 1, 3, norm[level], (0,))
        half_sweep(level, 0, 2)
        half_sweep(level, 1, 1)
        residual(level)

    barrier = pltpu.get_barrier_semaphore()
    fetch_inv = pltpu.make_async_copy(inv_hbm, inv_ref, load_sem.at[0])
    fetch_src = pltpu.make_async_copy(src_hbm, src_ref, load_sem.at[1])
    fetch_inv.start()
    fetch_src.start()
    for a, c in PARTNERS:
        pl.semaphore_signal(barrier, inc=1, device_id=device(a, c), device_id_type=MESH)

    wide = lax.broadcasted_iota(jnp.int32, (16, LANES), 1)

    def take(ref, to):
        def body(x, px):
            odd = odd_rows(16, px).astype(jnp.int32)
            low = wide < LANES // 2
            lower, upper = ref[x, :, pl.ds(0, LANES)], ref[x, :, pl.ds(LANES, LANES)]
            for c in (0, 1):
                slot = lax.rem(2 * wide + (odd if c == 0 else 1 - odd), LANES)
                value = jnp.where(low, jnp.take_along_axis(lower, slot, axis=1), jnp.take_along_axis(upper, slot, axis=1))
                to[c, HX[0] + x, pl.ds(HY[0], 16)] = value

        rows(0, 16, body, 16)

    fetch_inv.wait()
    take(inv_ref, beta[0])
    fetch_src.wait()
    take(src_ref, b[0])
    pl.semaphore_wait(barrier, len(PARTNERS))
    send("e0k")
    send("e0")
    send("b0")
    send("b0k")
    for level in (0, 1, 2):
        coarsen_beta(level)
    send("e1x")
    send("e2x")
    receive("e0k", "e0")
    set_up(0, 4, 8)
    receive("b0", "b0k")
    normalise(0, 4)
    descend(0)

    send("b1")
    receive("e1x", "e2x")
    send("e1y")
    send("e2y")
    send("b1x")
    send("e3x")
    send("f0x")
    keep_own(1, b1w)
    receive("e1y")
    set_up(1, 4, 8)
    receive("b1")
    normalise(1, 4)
    descend(1)

    send("b2")
    receive("e3x", "f0x", "b1x")
    send("e3y")
    send("f1x")
    send("b1y")
    keep_own(2, b2w)
    receive("e2y")
    set_up(2, 4, 6)
    receive("b2")
    normalise(2, 4)
    descend(2)

    send("b3")
    send("f2x")
    send("b2x")
    receive("f1x")
    send("f1y")
    send("f0y")
    receive("e3y")
    set_up(3, 6, 14)
    receive("b3")
    normalise(3, 6)
    half_sweep(3, 1, 5, norm[3], (0,))
    for step in range(2, 7):
        half_sweep(3, step % 2, 6 - step)
    for x in range(HX[3], HX[3] + N[3]):
        field[3][x, pl.ds(HY[3], N[3])] = red_p[3][x, pl.ds(HY[3], N[3])]
    send("f3")
    receive("f2x", "b2x")
    send("f2y")
    send("b2y")

    for name in NAMES:
        if name not in ("b2y", "f2y", "f3"):
            await_bytes(send_sem, name)
    set_up(1, 6, 4)
    set_up(2, 7, 6)
    receive("b1y")
    normalise(1, 6, b1w)
    receive("b2y")
    normalise(2, 7, b2w)
    receive("f3")
    half_sweep(3, 1, 5, field[3])

    receive("f2y")
    prolong(2, 0, 20, 2, 24, field[3])
    for step in range(4):
        half_sweep(2, step % 2, 7 - step)
    receive("f1y")
    prolong(1, 0, 24, 2, 24, red_p[2])
    for step in range(4):
        half_sweep(1, step % 2, 6 - step)
    receive("f0y")
    prolong(0, 2, 24, 2, 24, red_p[1])
    for step in range(4):
        half_sweep(0, step % 2, 3 - step)

    def give(x, px):
        red, black = red_p[0][HX[0] + x, pl.ds(HY[0], 16)], black_p[0][HX[0] + x, pl.ds(HY[0], 16)]
        is_red = (wide + odd_rows(16, px).astype(jnp.int32)) % 2 == 0
        for part in (0, 1):
            slot = wide // 2 + part * (LANES // 2)
            out_ref[x, :, pl.ds(part * LANES, LANES)] = jnp.where(
                is_red, jnp.take_along_axis(red, slot, axis=1), jnp.take_along_axis(black, slot, axis=1))

    rows(0, 16, give, 16)
    for name in ("b2y", "f2y", "f3"):
        await_bytes(send_sem, name)


def solution(mesh):
    gx_size, gy_size = mesh.shape["gx"], mesh.shape["gy"]

    def both(level):
        return pltpu.VMEM((2, XE[level], YE[level], LANES), jnp.float32)

    def single(level):
        return pltpu.VMEM((XE[level], YE[level], LANES), jnp.float32)

    levels = range(4)
    block = pltpu.VMEM((16, 16, 2 * LANES), jnp.float32)
    scratch = [both(level) for _ in range(3) for level in levels]
    scratch += [single(level) for _ in range(2) for level in levels]
    scratch += [pltpu.VMEM((7, 2, XE[level], YE[level], LANES), jnp.float32) for level in levels]
    scratch += [single(level) for level in range(3)] + [single(level) for level in levels]
    scratch += [both(1), both(2), pltpu.VMEM((16, 16, LANES), jnp.float32), block, block]
    scratch += [pltpu.VMEM((MOST, LANES), jnp.float32), pltpu.SemaphoreType.DMA((2,))]
    scratch += [pltpu.SemaphoreType.DMA((len(NAMES),))] * 2

    def on_device(source, inv_density):
        hbm = pl.BlockSpec(memory_space=pltpu.HBM)

        def body(*refs):
            kernel(gx_size, gy_size, *refs)

        return pl.pallas_call(
            body,
            out_shape=pltpu.VMEM(source.shape, jnp.float32),
            in_specs=[hbm, hbm],
            out_specs=pl.BlockSpec(memory_space=pltpu.VMEM),
            scratch_shapes=scratch,
            name="v_cycle",
            compiler_params=pltpu.CompilerParams(
                collective_id=0, has_side_effects=True, vmem_limit_bytes=60 << 20
            ),
        )(source, inv_density)

    placed = P("gx", "gy", None)
    return jax.shard_map(
        on_device, mesh=mesh, in_specs=(placed, placed), out_specs=placed, check_vma=False
    )
```
